32 devices in a mesh: gx: 2 (over x), gy: 4 (over y, core), gz: 4 (over z).
Axes of the slice: x: 2, y: 2, z: 4, core: 2. Of those that a mesh axis runs over, the one named last changes fastest.
Arguments:
- multipoles: bfloat16 [289, 16384], P(None, ('gx', 'gy', 'gz')), may hold values from -6 to 6
- up_shift: bfloat16 [8, 289, 289], replicated, may hold values from -0.125 to 0.125
- down_shift: bfloat16 [8, 289, 289], replicated, may hold values from -0.375 to 0.375
- far_shift: bfloat16 [8, 289, 289], replicated, may hold values from -0.09375 to 0.09375
- send_list: int32 [2, 16, 16, 16], P('gx', ('gy', 'gz')), may hold values from 0 to 511
- leaf_src: int32 [16, 16384], P(None, ('gx', 'gy', 'gz')), may hold values from 0 to 767
- leaf_kind: int32 [16, 16384], P(None, ('gx', 'gy', 'gz')), may hold values from 0 to 7
- coarse_src: int32 [8, 4], replicated, may hold values from 0 to 3
- coarse_kind: int32 [8, 4], replicated, may hold values from 0 to 7
Outputs:
- leaf_local: bfloat16 [289, 16384], P(None, ('gx', 'gy', 'gz'))
The draws below stay inside these ranges and needn't reach their ends.
All inputs are finite; a program needn't handle non-finite values.
Results may differ from the reference program's by a relative error of at most 0.014.
Values may be sent and summed in bfloat16 or wider, within the bound.
A program may use at most 128 MiB of HBM per device.

```python
import math
import jax
import jax.numpy as jnp
import numpy as np
from jax import lax

P2 = 289
LOCAL_LEVELS = 3
KINDS = 8
LIST = 16
CL = 8
SLOT = 16
LEAF_DEV = 512
PEERS = 16
LEAVES = 16384
NBUF = 768
COARSE = 4
N_GX = 2
N_GY = 4
N_GZ = 4


def with_ends(values, stream_key, least, largest):
    longest = values.shape.index(max(values.shape))
    spots = []
    for shift in (0, 1):
        where = [jax.random.randint(jax.random.fold_in(stream_key, axis), (), 0, length) for axis, length in enumerate(values.shape)]
        where[longest] = (where[longest] + shift) % values.shape[longest]
        spots.append(tuple(where))
    return values.at[spots[0]].set(least).at[spots[1]].set(largest)


def level_of(own_key, shape, cuts, smallest, top_value):
    def one(dim, blocks):
        draws = jax.random.uniform(jax.random.fold_in(jax.random.fold_in(own_key, 6), dim), (blocks,), jnp.float32, smallest / len(cuts), top_value / len(cuts))
        return jnp.repeat(jnp.exp(draws), shape[dim] // blocks).reshape((-1,) + (1,) * (len(shape) - dim - 1))

    loudness = one(*cuts[0])
    for cut in cuts[1:]:
        loudness = loudness * one(*cut)
    return loudness


def rank_bounds(number_of, skew):
    weights = [(1 << 20) // math.isqrt(rank ** skew) + 1 for rank in range(1, number_of + 1)]
    scale = 1 + sum(weights) // (1 << 30)
    return np.cumsum(np.array([max(1, weight // scale) for weight in weights]))


def skewed_ids(stream_key, shape, count, skew):
    listing = rank_bounds(count, skew)
    pick = jax.random.randint(jax.random.fold_in(stream_key, 1), shape, 0, int(listing[count - 1]))
    standing = jnp.searchsorted(jnp.asarray(listing, jnp.int32), pick, side="right")
    return jax.random.permutation(jax.random.fold_in(stream_key, 2), count)[standing].astype(jnp.int32)


def scatter_about(key, extent, scale, bound, cuts=(), held_as=jnp.bfloat16):
    values = scale * jax.random.normal(key, extent, jnp.float32)
    if cuts:
        values = values * level_of(key, extent, cuts, -0.22, 0.18)
    return jnp.clip(values, -bound, bound).astype(held_as)


def setup_inputs(seed: int = 0) -> dict:
    arg_keys = jax.random.split(jax.random.key(seed), 10)
    multipoles = scatter_about(arg_keys[0], (P2, LEAVES), 1.0, 6.0, ((1, 32),))
    up_shift = scatter_about(arg_keys[1], (8, P2, P2), (8 * P2) ** -0.5, 0.125)
    down_shift = scatter_about(arg_keys[2], (8, P2, P2), P2 ** -0.5, 0.375)
    far_shift = scatter_about(arg_keys[3], (KINDS, P2, P2), (LIST * P2) ** -0.5, 0.09375)
    send_list = with_ends(skewed_ids(arg_keys[4], (N_GX, PEERS, PEERS, SLOT), LEAF_DEV, 2), jax.random.fold_in(arg_keys[4], 3), 0, LEAF_DEV - 1).astype(jnp.int32)
    leaf_src = with_ends(jax.random.randint(arg_keys[5], (LIST, LEAVES), 0, NBUF), jax.random.fold_in(arg_keys[5], 1), 0, NBUF - 1).astype(jnp.int32)
    leaf_kind = with_ends(jax.random.randint(arg_keys[6], (LIST, LEAVES), 0, KINDS), jax.random.fold_in(arg_keys[6], 1), 0, KINDS - 1).astype(jnp.int32)
    coarse_src = with_ends(jax.random.randint(arg_keys[7], (CL, COARSE), 0, COARSE), jax.random.fold_in(arg_keys[7], 1), 0, COARSE - 1).astype(jnp.int32)
    coarse_kind = with_ends(jax.random.randint(arg_keys[8], (CL, COARSE), 0, KINDS), jax.random.fold_in(arg_keys[8], 1), 0, KINDS - 1).astype(jnp.int32)
    return {"multipoles": multipoles, "up_shift": up_shift, "down_shift": down_shift, "far_shift": far_shift, "send_list": send_list, "leaf_src": leaf_src, "leaf_kind": leaf_kind, "coarse_src": coarse_src, "coarse_kind": coarse_kind}


def lift_level(children, up_shift):
    count = children.shape[1] // 8
    child_stack = children.reshape(P2, count, 8).transpose(2, 0, 1).reshape(8 * P2, count)
    shift_table = up_shift.transpose(1, 0, 2).reshape(P2, 8 * P2)
    return jnp.dot(shift_table, child_stack, preferred_element_type=jnp.float32)


def lower_level(parent, down_shift):
    count = parent.shape[1]
    spread = jnp.dot(down_shift.reshape(8 * P2, P2), parent, preferred_element_type=jnp.float32)
    return spread.reshape(8, P2, count).transpose(1, 2, 0).reshape(P2, 8 * count)


def sum_by_kind(picked, kind_ids, far_shift):
    far_total = jnp.zeros((picked.shape[1], picked.shape[2]), jnp.float32)
    for kind in range(KINDS):
        kind_mask = (kind_ids == kind)[:, None, :]
        grouped = jnp.sum(jnp.where(kind_mask, picked.astype(jnp.float32), jnp.float32(0.0)), axis=0)
        far_total = far_total + jnp.dot(far_shift[kind].astype(jnp.float32), grouped, precision=lax.Precision.HIGHEST)
    return far_total


def reference(multipoles, up_shift, down_shift, far_shift, send_list, leaf_src, leaf_kind, coarse_src, coarse_kind):
    devices = N_GX * N_GY * N_GZ
    upward = multipoles
    for level in range(LOCAL_LEVELS):
        upward = lift_level(upward, up_shift).astype(jnp.bfloat16)
    coarse_multi = lift_level(upward, up_shift).astype(jnp.bfloat16)
    coarse_picked = coarse_multi[:, coarse_src].transpose(1, 0, 2)
    coarse_local = sum_by_kind(coarse_picked, coarse_kind, far_shift).astype(jnp.bfloat16)
    downward = lower_level(coarse_local, down_shift).astype(jnp.bfloat16)
    for level in range(LOCAL_LEVELS - 1):
        downward = lower_level(downward, down_shift).astype(jnp.bfloat16)
    chain_part = lower_level(downward, down_shift)

    def one_device(device):
        row_group = device // PEERS
        column = device % PEERS
        own_leaves = device * LEAF_DEV + jnp.arange(LEAF_DEV, dtype=jnp.int32)
        sent_rows = send_list[row_group, :, column, :]
        ghost_rows = (row_group * PEERS + jnp.arange(PEERS, dtype=jnp.int32))[:, None] * LEAF_DEV + sent_rows
        source_buffer = jnp.concatenate([own_leaves, ghost_rows.reshape(PEERS * SLOT).astype(jnp.int32)]).astype(jnp.int32)
        local_src = lax.dynamic_slice_in_dim(leaf_src, (device * LEAF_DEV).astype(jnp.int32), LEAF_DEV, 1)
        kind_ids = lax.dynamic_slice_in_dim(leaf_kind, (device * LEAF_DEV).astype(jnp.int32), LEAF_DEV, 1)
        global_src = source_buffer[local_src]
        picked = multipoles[:, global_src].transpose(1, 0, 2)
        return sum_by_kind(picked, kind_ids, far_shift)

    far = lax.map(one_device, jnp.arange(devices, dtype=jnp.int32))
    far = far.transpose(1, 0, 2).reshape(P2, devices * LEAF_DEV)
    return (chain_part + far).astype(jnp.bfloat16)
```

```python
import functools

import jax
import jax.numpy as jnp
from jax import lax
from jax.experimental import pallas as pl
from jax.experimental.pallas import tpu as pltpu
from jax.sharding import PartitionSpec as P

MESH = pl.DeviceIdType.MESH
LOCAL_LEVELS = 3
LANES = 128
ROWS = 64
FIELD = 15
LOW_NIBBLES = 0x0F0F0F0F
F32 = jnp.float32
BF16 = jnp.bfloat16


def iota(shape, dim):
    return lax.broadcasted_iota(jnp.int32, shape, dim)


def dot(a, b):
    return jnp.dot(a, b, preferred_element_type=F32)


def pick_children(rows):
    shape = (rows, 8 * LANES)
    col = iota(shape, 1)
    return (iota(shape, 0) == 8 * (col % LANES) + col // LANES).astype(F32).astype(BF16)


def spread_children():
    shape = (LANES, 8 * LANES)
    col = iota(shape, 1)
    place = col % LANES
    hit = (iota(shape, 0) == place // 8) & (place % 8 == col // LANES)
    return hit.astype(F32).astype(BF16)


def apply_eight(table, blocks):
    total = None
    for c in range(8):
        term = dot(table(c), blocks[:, c * LANES : (c + 1) * LANES])
        total = term if total is None else total + term
    return total


def kernel(
    sizes,
    mult_hbm,
    up_hbm,
    down_hbm,
    far_hbm,
    send_ref,
    src_ref,
    kind_ref,
    csrc_ref,
    ckind_ref,
    out_ref,
    mult,
    up,
    down,
    farw,
    sel,
    spread,
    out_rows,
    arrived,
    table,
    buf,
    far_total,
    turn,
    message,
    boxes,
    load_sem,
    a2a_send,
    a2a_recv,
    box_send,
    box_recv,
):
    n_gx, n_gy, n_gz = sizes
    peers = n_gy * n_gz
    devices = n_gx * peers
    gx = lax.axis_index("gx")
    q = lax.axis_index("gy") * n_gz + lax.axis_index("gz")
    me = gx * peers + q
    coefs, leaves = mult.shape
    slots = send_ref.shape[1]
    kinds = farw.shape[0]
    sources = table.shape[1]
    list_len = src_ref.shape[0]

    loads = [
        pltpu.make_async_copy(a, b, load_sem.at[i])
        for i, (a, b) in enumerate(
            ((mult_hbm, mult), (up_hbm, up), (far_hbm, farw), (down_hbm, down))
        )
    ]
    for load in loads:
        load.start()

    def device_of(flat):
        return (flat // peers, (flat % peers) // n_gz, flat % n_gz)

    barrier = pltpu.get_barrier_semaphore()

    def greet(i, carry):
        pl.semaphore_signal(
            barrier, inc=1, device_id=device_of((me + i) % devices), device_id_type=MESH
        )
        return carry

    lax.fori_loop(1, devices, greet, 0)

    count = peers * slots
    row_of = (iota((count, peers), 0) // slots == iota((count, peers), 1)).astype(F32).astype(BF16)
    wanted = send_ref[...]
    upper = dot(row_of, (wanted // 32).astype(F32).astype(BF16))
    lower = dot(row_of, (wanted % 32).astype(F32).astype(BF16))
    mine = iota((count, slots), 0) % slots == iota((count, slots), 1)
    leaf = jnp.sum(jnp.where(mine, upper * 32.0 + lower, 0.0), axis=1, keepdims=True)
    hot = (leaf.astype(jnp.int32) == iota((count, leaves), 1)).astype(F32).astype(BF16)
    sel[...] = pick_children(leaves)
    spread[...] = spread_children()
    out_rows[...] = jnp.zeros_like(out_rows)
    loads[0].wait()
    out_rows[:, :coefs] = lax.dot_general(
        hot, mult[...], (((1,), (1,)), ((), ())), preferred_element_type=F32
    ).astype(BF16)
    own = pl.ds(pl.multiple_of(q * slots, slots), slots)
    arrived[own, :] = out_rows[own, :]

    pl.semaphore_wait(barrier, devices - 1)

    def send_rows(i, carry):
        other = (q + i) % peers
        pltpu.make_async_remote_copy(
            src_ref=out_rows.at[pl.ds(pl.multiple_of(other * slots, slots), slots)],
            dst_ref=arrived.at[own],
            send_sem=a2a_send,
            recv_sem=a2a_recv,
            device_id=(gx, other // n_gz, other % n_gz),
            device_id_type=MESH,
        ).start()
        return carry

    lax.fori_loop(1, peers, send_rows, 0)

    loads[1].wait()
    turn[...] = jnp.zeros_like(turn)
    x = mult[...]
    for level in range(LOCAL_LEVELS):
        picked = dot(x, sel[: x.shape[1], :]).astype(BF16)
        total = apply_eight(lambda c: up[c], picked)
        x = total.astype(BF16)
    turn[:coefs, :] = x.astype(F32)
    row = turn[...].T[0:1, :]
    message[...] = row
    boxes[me] = row

    def send_box(i, carry):
        pltpu.make_async_remote_copy(
            src_ref=message,
            dst_ref=boxes.at[me],
            send_sem=box_send,
            recv_sem=box_recv,
            device_id=device_of((me + i) % devices),
            device_id_type=MESH,
        ).start()
        return carry

    lax.fori_loop(1, devices, send_box, 0)

    def count_rows(step, carry):
        s0 = pl.multiple_of(step * ROWS, ROWS)
        for lane in range(0, leaves, LANES):
            cols = slice(lane, lane + LANES)
            sid = iota((ROWS, LANES), 0) + s0
            parts = []
            for start in range(0, list_len, FIELD):
                acc = jnp.zeros((ROWS, LANES), jnp.int32)
                for j in range(start, min(start + FIELD, list_len)):
                    weight = lax.shift_left(jnp.int32(1), 4 * kind_ref[j : j + 1, cols])
                    acc = acc + jnp.where(src_ref[j : j + 1, cols] == sid, weight, 0)
                parts.append(acc)
            even = sum(a & LOW_NIBBLES for a in parts)
            odd = sum(lax.shift_right_logical(a, 4) & LOW_NIBBLES for a in parts)
            for k in range(kinds):
                word = odd if k % 2 else even
                field = lax.shift_right_logical(word, 8 * (k // 2)) & 255
                table[k, pl.ds(s0, ROWS), cols] = field.astype(F32).astype(BF16)
        return carry

    lax.fori_loop(0, sources // ROWS, count_rows, 0)

    buf[:, :leaves] = mult[...]
    part = arrived.at[pl.ds(0, (peers - 1) * slots)]
    pltpu.make_async_copy(part, part, a2a_recv).wait()
    buf[:, leaves:] = arrived[...].astype(F32).T[:coefs, :].astype(BF16)
    loads[2].wait()
    far_total[...] = jnp.zeros_like(far_total)

    def add_kind(k, carry):
        grouped = dot(buf[...], table[k]).astype(BF16)
        far_total[...] += dot(farw[k], grouped)
        return carry

    lax.fori_loop(0, kinds, add_kind, 0)

    part = boxes.at[pl.ds(0, devices - 1)]
    pltpu.make_async_copy(part, part, box_recv).wait()
    x = boxes[...].reshape(devices, boxes.shape[2]).T[:coefs, :].astype(BF16)
    picked = dot(x, sel[:devices, :]).astype(BF16)
    coarse = apply_eight(lambda c: up[c], picked).astype(BF16)
    box = me // 8
    total = None
    for j in range(csrc_ref.shape[0]):
        hit = (iota((LANES, LANES), 0) == csrc_ref[j, box]) & (iota((LANES, LANES), 1) == 0)
        picked = dot(coarse, hit.astype(F32).astype(BF16)).astype(BF16)
        term = dot(farw[ckind_ref[j, box]], picked)
        total = term if total is None else total + term
    x = total.astype(BF16)

    loads[3].wait()
    x = dot(down[me % 8], x).astype(BF16)
    for level in range(LOCAL_LEVELS - 1):
        picked = dot(x, spread[...]).astype(BF16)
        x = apply_eight(lambda c: down[c], picked).astype(BF16)
    half = LANES // 2
    shape = (LANES, LANES)
    shift = ((iota(shape, 0) + half == iota(shape, 1)) & (iota(shape, 0) < half)).astype(F32)
    shifted = dot(x, shift.astype(BF16)).astype(BF16)
    result = far_total[...]
    for pair in range(4):
        chain = dot(down[2 * pair], x) + dot(down[2 * pair + 1], shifted)
        upper = chain.astype(BF16)
        lower = (chain - upper.astype(F32)).astype(BF16)
        place = iota((LANES, leaves), 0)
        goes = 8 * (place % half) + place // half + 2 * pair
        spot = (goes == iota((LANES, leaves), 1)).astype(F32).astype(BF16)
        result = result + dot(upper, spot) + dot(lower, spot)
    out_ref[...] = result.astype(BF16)

    part = out_rows.at[pl.ds(0, (peers - 1) * slots)]
    pltpu.make_async_copy(part, part, a2a_send).wait()
    part = boxes.at[pl.ds(0, devices - 1)]
    pltpu.make_async_copy(part, part, box_send).wait()


def solution(mesh):
    sizes = (mesh.shape["gx"], mesh.shape["gy"], mesh.shape["gz"])
    peers = sizes[1] * sizes[2]
    devices = sizes[0] * peers

    def on_device(mult, up, down, farw, send, src, kind, csrc, ckind):
        coefs, leaves = mult.shape
        kinds = farw.shape[0]
        slots = send.shape[3]
        sources = leaves + peers * slots
        wide = -(-coefs // LANES) * LANES
        vmem = pl.BlockSpec(memory_space=pltpu.VMEM)
        smem = pl.BlockSpec(memory_space=pltpu.SMEM)
        hbm = pl.BlockSpec(memory_space=pl.ANY)
        return pl.pallas_call(
            functools.partial(kernel, sizes),
            out_shape=jax.ShapeDtypeStruct((coefs, leaves), BF16),
            in_specs=[hbm] * 4 + [vmem] * 3 + [smem] * 2,
            out_specs=vmem,
            scratch_shapes=[
                pltpu.VMEM(mult.shape, BF16),
                pltpu.VMEM(up.shape, BF16),
                pltpu.VMEM(down.shape, BF16),
                pltpu.VMEM(farw.shape, BF16),
                pltpu.VMEM((leaves, 8 * LANES), BF16),
                pltpu.VMEM((LANES, 8 * LANES), BF16),
                pltpu.VMEM((peers * slots, wide), BF16),
                pltpu.VMEM((peers * slots, wide), BF16),
                pltpu.VMEM((kinds, sources, leaves), BF16),
                pltpu.VMEM((coefs, sources), BF16),
                pltpu.VMEM((coefs, leaves), F32),
                pltpu.VMEM((wide, LANES), F32),
                pltpu.VMEM((1, wide), F32),
                pltpu.VMEM((devices, 1, wide), F32),
                pltpu.SemaphoreType.DMA((4,)),
                pltpu.SemaphoreType.DMA,
                pltpu.SemaphoreType.DMA,
                pltpu.SemaphoreType.DMA,
                pltpu.SemaphoreType.DMA,
            ],
            compiler_params=pltpu.CompilerParams(
                collective_id=0, has_side_effects=True, vmem_limit_bytes=50 * 2**20
            ),
        )(mult, up, down, farw, send.reshape(peers, slots), src, kind, csrc, ckind)

    leaf = P(None, ("gx", "gy", "gz"))
    in_specs = (leaf, P(), P(), P(), P("gx", ("gy", "gz"), None, None), leaf, leaf, P(), P())
    return jax.shard_map(
        on_device, mesh=mesh, in_specs=in_specs, out_specs=leaf, check_vma=False
    )
```

```python
import functools

import jax
import jax.numpy as jnp
from jax import lax
from jax.experimental import pallas as pl
from jax.experimental.pallas import tpu as pltpu
from jax.sharding import PartitionSpec as P

MESH = pl.DeviceIdType.MESH
LOCAL_LEVELS = 3
LANES = 128
ROWS = 64
BLOCK = 32
FIELD = 15
LOW_NIBBLES = 0x0F0F0F0F
F32 = jnp.float32
BF16 = jnp.bfloat16


def iota(shape, dim):
    return lax.broadcasted_iota(jnp.int32, shape, dim)


def dot(a, b):
    return jnp.dot(a, b, preferred_element_type=F32)


def pick_children(rows):
    shape = (rows, 8 * LANES)
    col = iota(shape, 1)
    return (iota(shape, 0) == 8 * (col % LANES) + col // LANES).astype(F32).astype(BF16)


def spread_children():
    shape = (LANES, 8 * LANES)
    col = iota(shape, 1)
    place = col % LANES
    hit = (iota(shape, 0) == place // 8) & (place % 8 == col // LANES)
    return hit.astype(F32).astype(BF16)


def apply_eight(table, blocks):
    total = None
    for c in range(8):
        term = dot(table(c), blocks[:, c * LANES : (c + 1) * LANES])
        total = term if total is None else total + term
    return total


def split_octants(raw, table, step):
    shape = (8 * BLOCK, 8 * BLOCK)
    to, frm = iota(shape, 0), iota(shape, 1)
    order = (frm == 8 * (to % BLOCK) + to // BLOCK).astype(F32).astype(BF16)
    rows = raw[pl.ds(pl.multiple_of(step * 8 * BLOCK, 8 * BLOCK), 8 * BLOCK), :]
    out = dot(order, rows).astype(BF16)
    for c in range(8):
        spot = pl.ds(pl.multiple_of(step * BLOCK, BLOCK), BLOCK)
        table[c, spot, :] = out[c * BLOCK : (c + 1) * BLOCK]


def split_tail(raw, table):
    coefs = raw.shape[0] // 8
    done = coefs // BLOCK * BLOCK
    left = coefs - done
    room = table.shape[1] - done
    shape = (8 * room, 8 * left)
    to, frm = iota(shape, 0), iota(shape, 1)
    hit = (frm == 8 * (to % room) + to // room) & (to % room < left)
    out = dot(hit.astype(F32).astype(BF16), raw[8 * done :, :]).astype(BF16)
    for c in range(8):
        table[c, done:, :] = out[c * room : (c + 1) * room]


def kernel(
    sizes,
    mult_hbm,
    up_hbm,
    down_hbm,
    far_hbm,
    send_ref,
    src_ref,
    kind_ref,
    csrc_ref,
    ckind_ref,
    out_ref,
    mult,
    up_raw,
    down_raw,
    far_raw,
    up,
    down,
    farw,
    sel,
    spread,
    out_rows,
    arrived,
    table,
    buf,
    far_total,
    turn,
    message,
    boxes,
    load_sem,
    a2a_send,
    a2a_recv,
    box_send,
    box_recv,
):
    n_gx, n_gy, n_gz = sizes
    peers = n_gy * n_gz
    devices = n_gx * peers
    gx = lax.axis_index("gx")
    q = lax.axis_index("gy") * n_gz + lax.axis_index("gz")
    me = gx * peers + q
    coefs, leaves = mult.shape
    slots = send_ref.shape[1]
    kinds = farw.shape[0]
    sources = table.shape[1]
    list_len = src_ref.shape[0]

    loads = [
        pltpu.make_async_copy(a, b, load_sem.at[i])
        for i, (a, b) in enumerate(
            ((up_hbm, up_raw), (mult_hbm, mult), (far_hbm, far_raw), (down_hbm, down_raw))
        )
    ]
    for load in loads:
        load.start()

    def device_of(flat):
        return (flat // peers, (flat % peers) // n_gz, flat % n_gz)

    barrier = pltpu.get_barrier_semaphore()

    def greet(i, carry):
        pl.semaphore_signal(
            barrier, inc=1, device_id=device_of((me + i) % devices), device_id_type=MESH
        )
        return carry

    lax.fori_loop(1, devices, greet, 0)

    sel[...] = pick_children(leaves)
    spread[...] = spread_children()
    blocks = coefs // BLOCK
    loads[0].wait()

    def split_up(i, carry):
        split_octants(up_raw, up, i)
        return carry

    lax.fori_loop(0, blocks, split_up, 0)
    split_tail(up_raw, up)
    loads[1].wait()
    turn[...] = jnp.zeros_like(turn)
    x = mult[...]
    for level in range(LOCAL_LEVELS):
        picked = dot(x, sel[: x.shape[1], :]).astype(BF16)
        total = apply_eight(lambda c: up[c, :coefs, :], picked)
        x = total.astype(BF16)
    turn[:coefs, :] = x.astype(F32)
    row = turn[...].T[0:1, :]
    message[...] = row
    boxes[me] = row

    count = peers * slots
    row_of = (iota((count, peers), 0) // slots == iota((count, peers), 1)).astype(F32).astype(BF16)
    wanted = send_ref[...]
    upper = dot(row_of, (wanted // 32).astype(F32).astype(BF16))
    lower = dot(row_of, (wanted % 32).astype(F32).astype(BF16))
    mine = iota((count, slots), 0) % slots == iota((count, slots), 1)
    leaf = jnp.sum(jnp.where(mine, upper * 32.0 + lower, 0.0), axis=1, keepdims=True)
    hot = (leaf.astype(jnp.int32) == iota((count, leaves), 1)).astype(F32).astype(BF16)
    out_rows[...] = jnp.zeros_like(out_rows)
    out_rows[:, :coefs] = lax.dot_general(
        hot, mult[...], (((1,), (1,)), ((), ())), preferred_element_type=F32
    ).astype(BF16)
    own = pl.ds(pl.multiple_of(q * slots, slots), slots)
    arrived[own, :] = out_rows[own, :]

    pl.semaphore_wait(barrier, devices - 1)

    def send_box(i, carry):
        pltpu.make_async_remote_copy(
            src_ref=message,
            dst_ref=boxes.at[me],
            send_sem=box_send,
            recv_sem=box_recv,
            device_id=device_of((me + i) % devices),
            device_id_type=MESH,
        ).start()
        return carry

    lax.fori_loop(1, devices, send_box, 0)

    def send_rows(i, carry):
        other = (q + i) % peers
        pltpu.make_async_remote_copy(
            src_ref=out_rows.at[pl.ds(pl.multiple_of(other * slots, slots), slots)],
            dst_ref=arrived.at[own],
            send_sem=a2a_send,
            recv_sem=a2a_recv,
            device_id=(gx, other // n_gz, other % n_gz),
            device_id_type=MESH,
        ).start()
        return carry

    lax.fori_loop(1, peers, send_rows, 0)

    def count_rows(step, carry):
        s0 = pl.multiple_of(step * ROWS, ROWS)
        for lane in range(0, leaves, LANES):
            cols = slice(lane, lane + LANES)
            sid = iota((ROWS, LANES), 0) + s0
            parts = []
            for start in range(0, list_len, FIELD):
                acc = jnp.zeros((ROWS, LANES), jnp.int32)
                for j in range(start, min(start + FIELD, list_len)):
                    weight = lax.shift_left(jnp.int32(1), 4 * kind_ref[j : j + 1, cols])
                    acc = acc + jnp.where(src_ref[j : j + 1, cols] == sid, weight, 0)
                parts.append(acc)
            even = sum(a & LOW_NIBBLES for a in parts)
            odd = sum(lax.shift_right_logical(a, 4) & LOW_NIBBLES for a in parts)
            for k in range(kinds):
                word = odd if k % 2 else even
                field = lax.shift_right_logical(word, 8 * (k // 2)) & 255
                table[k, pl.ds(s0, ROWS), cols] = field.astype(F32).astype(BF16)
        return carry

    def count_and_split(step, carry):
        split_octants(far_raw, farw, step)
        split_octants(down_raw, down, step)
        return count_rows(step, carry)

    loads[2].wait()
    loads[3].wait()
    both = min(blocks, sources // ROWS)
    assert both == blocks
    lax.fori_loop(0, both, count_and_split, 0)
    lax.fori_loop(both, sources // ROWS, count_rows, 0)
    split_tail(far_raw, farw)
    split_tail(down_raw, down)

    buf[:, :leaves] = mult[...]
    part = arrived.at[pl.ds(0, (peers - 1) * slots)]
    pltpu.make_async_copy(part, part, a2a_recv).wait()
    buf[:, leaves:] = arrived[...].astype(F32).T[:coefs, :].astype(BF16)
    part = boxes.at[pl.ds(0, devices - 1)]
    pltpu.make_async_copy(part, part, box_recv).wait()
    far_total[...] = jnp.zeros_like(far_total)

    def add_kinds(which):
        for k in which:
            grouped = dot(buf[...], table[k]).astype(BF16)
            far_total[...] += dot(farw[k, :coefs, :], grouped)

    turns = [range(t * kinds // 4, (t + 1) * kinds // 4) for t in range(4)]

    x = boxes[...].reshape(devices, boxes.shape[2]).T[:coefs, :].astype(BF16)
    picked = dot(x, sel[:devices, :]).astype(BF16)
    coarse = apply_eight(lambda c: up[c, :coefs, :], picked).astype(BF16)
    add_kinds(turns[0])
    box = me // 8
    total = None
    for j in range(csrc_ref.shape[1]):
        hit = (iota((LANES, LANES), 0) == csrc_ref[box, j]) & (iota((LANES, LANES), 1) == 0)
        picked = dot(coarse, hit.astype(F32).astype(BF16)).astype(BF16)
        term = dot(farw[ckind_ref[box, j], :coefs, :], picked)
        total = term if total is None else total + term
    x = total.astype(BF16)
    add_kinds(turns[1])

    x = dot(down[me % 8, :coefs, :], x).astype(BF16)
    for level in range(LOCAL_LEVELS - 1):
        picked = dot(x, spread[...]).astype(BF16)
        x = apply_eight(lambda c: down[c, :coefs, :], picked).astype(BF16)
        add_kinds(turns[2 + level])
    half = LANES // 2
    shape = (LANES, LANES)
    shift = ((iota(shape, 0) + half == iota(shape, 1)) & (iota(shape, 0) < half)).astype(F32)
    shifted = dot(x, shift.astype(BF16)).astype(BF16)
    result = far_total[...]
    for pair in range(4):
        chain = dot(down[2 * pair, :coefs, :], x) + dot(down[2 * pair + 1, :coefs, :], shifted)
        upper = chain.astype(BF16)
        lower = (chain - upper.astype(F32)).astype(BF16)
        place = iota((LANES, leaves), 0)
        goes = 8 * (place % half) + place // half + 2 * pair
        spot = (goes == iota((LANES, leaves), 1)).astype(F32).astype(BF16)
        result = result + dot(upper, spot) + dot(lower, spot)
    out_ref[...] = result.astype(BF16)

    part = out_rows.at[pl.ds(0, (peers - 1) * slots)]
    pltpu.make_async_copy(part, part, a2a_send).wait()
    part = boxes.at[pl.ds(0, devices - 1)]
    pltpu.make_async_copy(part, part, box_send).wait()


def solution(mesh):
    sizes = (mesh.shape["gx"], mesh.shape["gy"], mesh.shape["gz"])
    peers = sizes[1] * sizes[2]
    devices = sizes[0] * peers

    def rows(table):
        return table.transpose(1, 0, 2).reshape(-1, table.shape[2])

    def on_device(mult, up, down, farw, send, src, kind, csrc, ckind):
        coefs, leaves = mult.shape
        kinds = farw.shape[0]
        slots = send.shape[3]
        sources = leaves + peers * slots
        tall = -(-coefs // 16) * 16
        wide = -(-coefs // LANES) * LANES
        vmem = pl.BlockSpec(memory_space=pltpu.VMEM)
        smem = pl.BlockSpec(memory_space=pltpu.SMEM)
        hbm = pl.BlockSpec(memory_space=pl.ANY)
        return pl.pallas_call(
            functools.partial(kernel, sizes),
            out_shape=jax.ShapeDtypeStruct((coefs, leaves), BF16),
            in_specs=[hbm] * 4 + [vmem] * 3 + [smem] * 2,
            out_specs=vmem,
            scratch_shapes=[
                pltpu.VMEM(mult.shape, BF16),
                pltpu.VMEM((8 * coefs, coefs), BF16),
                pltpu.VMEM((8 * coefs, coefs), BF16),
                pltpu.VMEM((8 * coefs, coefs), BF16),
                pltpu.VMEM((8, tall, coefs), BF16),
                pltpu.VMEM((8, tall, coefs), BF16),
                pltpu.VMEM((8, tall, coefs), BF16),
                pltpu.VMEM((leaves, 8 * LANES), BF16),
                pltpu.VMEM((LANES, 8 * LANES), BF16),
                pltpu.VMEM((peers * slots, wide), BF16),
                pltpu.VMEM((peers * slots, wide), BF16),
                pltpu.VMEM((kinds, sources, leaves), BF16),
                pltpu.VMEM((coefs, sources), BF16),
                pltpu.VMEM((coefs, leaves), F32),
                pltpu.VMEM((wide, LANES), F32),
                pltpu.VMEM((1, wide), F32),
                pltpu.VMEM((devices, 1, wide), F32),
                pltpu.SemaphoreType.DMA((4,)),
                pltpu.SemaphoreType.DMA,
                pltpu.SemaphoreType.DMA,
                pltpu.SemaphoreType.DMA,
                pltpu.SemaphoreType.DMA,
            ],
            compiler_params=pltpu.CompilerParams(
                collective_id=0, has_side_effects=True, vmem_limit_bytes=50 * 2**20
            ),
        )(
            mult,
            rows(up),
            rows(down),
            rows(farw),
            send.reshape(peers, slots),
            src,
            kind,
            csrc.T,
            ckind.T,
        )

    leaf = P(None, ("gx", "gy", "gz"))
    in_specs = (leaf, P(), P(), P(), P("gx", ("gy", "gz"), None, None), leaf, leaf, P(), P())
    return jax.shard_map(
        on_device, mesh=mesh, in_specs=in_specs, out_specs=leaf, check_vma=False
    )
```

```python
import functools

import jax
import jax.numpy as jnp
from jax import lax
from jax.experimental import pallas as pl
from jax.experimental.pallas import tpu as pltpu
from jax.sharding import PartitionSpec as P

MESH = pl.DeviceIdType.MESH
LOCAL_LEVELS = 3
LANES = 128
ROWS = 64
BLOCK = 32
FIELD = 15
LOW_NIBBLES = 0x0F0F0F0F
F32 = jnp.float32
BF16 = jnp.bfloat16


def iota(shape, dim):
    return lax.broadcasted_iota(jnp.int32, shape, dim)


def dot(a, b):
    return jnp.dot(a, b, preferred_element_type=F32)


def pick_children(rows):
    shape = (rows, 8 * LANES)
    col = iota(shape, 1)
    return (iota(shape, 0) == 8 * (col % LANES) + col // LANES).astype(F32).astype(BF16)


def spread_children():
    shape = (LANES, 8 * LANES)
    col = iota(shape, 1)
    place = col % LANES
    hit = (iota(shape, 0) == place // 8) & (place % 8 == col // LANES)
    return hit.astype(F32).astype(BF16)


def stack_two(first, second, depth):
    gap = jnp.zeros((depth // 2 - first.shape[0], first.shape[1]), BF16)
    return jnp.concatenate([first, gap, second, gap], axis=0)


def apply_eight(table, blocks):
    total = None
    for pair in range(4):
        first = blocks[:, 2 * pair * LANES : (2 * pair + 1) * LANES]
        second = blocks[:, (2 * pair + 1) * LANES : (2 * pair + 2) * LANES]
        term = dot(table[pair], stack_two(first, second, table.shape[2]))
        total = term if total is None else total + term
    return total


def split_octants(raw, table, step):
    shape = (8 * BLOCK, 8 * BLOCK)
    to, frm = iota(shape, 0), iota(shape, 1)
    order = (frm == 8 * (to % BLOCK) + to // BLOCK).astype(F32).astype(BF16)
    rows = raw[pl.ds(pl.multiple_of(step * 8 * BLOCK, 8 * BLOCK), 8 * BLOCK), :]
    out = dot(order, rows).astype(BF16)
    for c in range(8):
        spot = pl.ds(pl.multiple_of(step * BLOCK, BLOCK), BLOCK)
        at = c % 2 * (table.shape[2] // 2)
        table[c // 2, spot, at : at + out.shape[1]] = out[c * BLOCK : (c + 1) * BLOCK]


def split_tail(raw, table):
    coefs = raw.shape[0] // 8
    done = coefs // BLOCK * BLOCK
    left = coefs - done
    room = table.shape[1] - done
    shape = (8 * room, 8 * left)
    to, frm = iota(shape, 0), iota(shape, 1)
    hit = (frm == 8 * (to % room) + to // room) & (to % room < left)
    out = dot(hit.astype(F32).astype(BF16), raw[8 * done :, :]).astype(BF16)
    for c in range(8):
        at = c % 2 * (table.shape[2] // 2)
        table[c // 2, done:, at : at + out.shape[1]] = out[c * room : (c + 1) * room]


def kernel(
    sizes,
    mult_hbm,
    up_hbm,
    down_hbm,
    far_hbm,
    send_hbm,
    src_hbm,
    kind_hbm,
    csrc_hbm,
    ckind_hbm,
    out_ref,
    send_ref,
    src_ref,
    kind_ref,
    csrc_ref,
    ckind_ref,
    mult,
    up_raw,
    down_raw,
    far_raw,
    up,
    down,
    farw,
    sel,
    spread,
    out_rows,
    arrived,
    table,
    buf,
    far_total,
    turn,
    coarse_hot,
    message,
    boxes,
    load_sem,
    a2a_send,
    a2a_recv,
    box_send,
    box_recv,
):
    n_gx, n_gy, n_gz = sizes
    peers = n_gy * n_gz
    devices = n_gx * peers
    gx = lax.axis_index("gx")
    q = lax.axis_index("gy") * n_gz + lax.axis_index("gz")
    me = gx * peers + q
    coefs, leaves = mult.shape
    slots = send_ref.shape[1]
    kinds = table.shape[0]
    sources = table.shape[1]
    list_len = src_ref.shape[0]

    loads = [
        pltpu.make_async_copy(a, b, load_sem.at[i])
        for i, (a, b) in enumerate(
            (
                (up_hbm, up_raw),
                (mult_hbm, mult),
                (send_hbm, send_ref),
                (src_hbm, src_ref),
                (kind_hbm, kind_ref),
                (csrc_hbm, csrc_ref),
                (ckind_hbm, ckind_ref),
                (far_hbm, far_raw),
                (down_hbm, down_raw),
            )
        )
    ]
    for load in loads:
        load.start()

    def device_of(flat):
        return (flat // peers, (flat % peers) // n_gz, flat % n_gz)

    barrier = pltpu.get_barrier_semaphore()

    def greet(i, carry):
        pl.semaphore_signal(
            barrier, inc=1, device_id=device_of((me + i) % devices), device_id_type=MESH
        )
        return carry

    lax.fori_loop(1, devices, greet, 0)

    sel[...] = pick_children(leaves)
    spread[...] = spread_children()
    blocks = coefs // BLOCK
    half_depth = up.shape[2] // 2
    for one in (up, farw, down):
        for end in (half_depth, 2 * half_depth):
            one[:, :, end - LANES : end] = jnp.zeros(one.shape[:2] + (LANES,), BF16)
    buf[...] = jnp.zeros_like(buf)
    loads[0].wait()

    def split_up(i, carry):
        split_octants(up_raw, up, i)
        return carry

    lax.fori_loop(0, blocks, split_up, 0)
    split_tail(up_raw, up)
    loads[1].wait()
    turn[...] = jnp.zeros_like(turn)
    buf[:coefs, :leaves] = mult[...]
    x = buf[:, :leaves]
    for level in range(LOCAL_LEVELS):
        picked = dot(x, sel[: x.shape[1], :]).astype(BF16)
        total = apply_eight(up, picked)
        x = total.astype(BF16)
    turn[: x.shape[0], :] = x.astype(F32)
    row = turn[...].T[0:1, :]
    message[...] = row
    boxes[me] = row

    loads[2].wait()
    count = peers * slots
    row_of = (iota((count, peers), 0) // slots == iota((count, peers), 1)).astype(F32).astype(BF16)
    wanted = send_ref[...]
    upper = dot(row_of, (wanted // 32).astype(F32).astype(BF16))
    lower = dot(row_of, (wanted % 32).astype(F32).astype(BF16))
    mine = iota((count, slots), 0) % slots == iota((count, slots), 1)
    leaf = jnp.sum(jnp.where(mine, upper * 32.0 + lower, 0.0), axis=1, keepdims=True)
    hot = (leaf.astype(jnp.int32) == iota((count, leaves), 1)).astype(F32).astype(BF16)
    out_rows[...] = jnp.zeros_like(out_rows)
    out_rows[:, :coefs] = lax.dot_general(
        hot, mult[...], (((1,), (1,)), ((), ())), preferred_element_type=F32
    ).astype(BF16)
    own = pl.ds(pl.multiple_of(q * slots, slots), slots)
    arrived[own, :] = out_rows[own, :]

    pl.semaphore_wait(barrier, devices - 1)

    def send_box(i, carry):
        pltpu.make_async_remote_copy(
            src_ref=message,
            dst_ref=boxes.at[me],
            send_sem=box_send,
            recv_sem=box_recv,
            device_id=device_of((me + i) % devices),
            device_id_type=MESH,
        ).start()
        return carry

    lax.fori_loop(1, devices, send_box, 0)

    def send_rows(i, carry):
        other = (q + i) % peers
        pltpu.make_async_remote_copy(
            src_ref=out_rows.at[pl.ds(pl.multiple_of(other * slots, slots), slots)],
            dst_ref=arrived.at[own],
            send_sem=a2a_send,
            recv_sem=a2a_recv,
            device_id=(gx, other // n_gz, other % n_gz),
            device_id_type=MESH,
        ).start()
        return carry

    lax.fori_loop(1, peers, send_rows, 0)

    def count_rows(step, carry):
        s0 = pl.multiple_of(step * ROWS, ROWS)
        for lane in range(0, leaves, LANES):
            cols = slice(lane, lane + LANES)
            sid = iota((ROWS, LANES), 0) + s0
            parts = []
            for start in range(0, list_len, FIELD):
                acc = jnp.zeros((ROWS, LANES), jnp.int32)
                for j in range(start, min(start + FIELD, list_len)):
                    weight = lax.shift_left(jnp.int32(1), 4 * kind_ref[j : j + 1, cols])
                    acc = acc + jnp.where(src_ref[j : j + 1, cols] == sid, weight, 0)
                parts.append(acc)
            even = sum(a & LOW_NIBBLES for a in parts)
            odd = sum(lax.shift_right_logical(a, 4) & LOW_NIBBLES for a in parts)
            for k in range(kinds):
                word = odd if k % 2 else even
                field = lax.shift_right_logical(word, 8 * (k // 2)) & 255
                table[k, pl.ds(s0, ROWS), cols] = field.astype(F32).astype(BF16)
        return carry

    def count_and_split(step, carry):
        split_octants(far_raw, farw, step)
        split_octants(down_raw, down, step)
        return count_rows(step, carry)

    for load in loads[3:]:
        load.wait()
    both = min(blocks, sources // ROWS)
    assert both == blocks
    lax.fori_loop(0, both, count_and_split, 0)
    lax.fori_loop(both, sources // ROWS, count_rows, 0)
    split_tail(far_raw, farw)
    split_tail(down_raw, down)

    box = me // 8
    total = jnp.zeros(coarse_hot.shape, jnp.int32)
    for j in range(csrc_ref.shape[1]):
        hit = (iota(total.shape, 0) == csrc_ref[box, j]) & (
            iota(total.shape, 1) == ckind_ref[box, j] * LANES
        )
        total = total + jnp.where(hit, 1, 0)
    coarse_hot[...] = total.astype(F32).astype(BF16)

    part = arrived.at[pl.ds(0, (peers - 1) * slots)]
    pltpu.make_async_copy(part, part, a2a_recv).wait()
    buf[:coefs, leaves:] = arrived[...].astype(F32).T[:coefs, :].astype(BF16)
    part = boxes.at[pl.ds(0, devices - 1)]
    pltpu.make_async_copy(part, part, box_recv).wait()
    far_total[...] = jnp.zeros_like(far_total)

    def add_kinds(which):
        for pair in which:
            first = dot(buf[...], table[2 * pair]).astype(BF16)
            second = dot(buf[...], table[2 * pair + 1]).astype(BF16)
            far_total[...] += dot(farw[pair], stack_two(first, second, farw.shape[2]))

    turns = [range(t * kinds // 8, (t + 1) * kinds // 8) for t in range(4)]

    x = boxes[...].reshape(devices, boxes.shape[2]).T[: buf.shape[0], :].astype(BF16)
    picked = dot(x, sel[:devices, :]).astype(BF16)
    coarse = apply_eight(up, picked).astype(BF16)
    add_kinds(turns[0])
    picked = dot(coarse, coarse_hot[...]).astype(BF16)
    x = apply_eight(farw, picked).astype(BF16)
    add_kinds(turns[1])

    octant = me % 8
    none = jnp.zeros_like(x)
    is_odd = octant % 2 == 1
    both = stack_two(jnp.where(is_odd, none, x), jnp.where(is_odd, x, none), down.shape[2])
    x = dot(down[octant // 2], both).astype(BF16)
    for level in range(LOCAL_LEVELS - 1):
        picked = dot(x, spread[...]).astype(BF16)
        x = apply_eight(down, picked).astype(BF16)
        add_kinds(turns[2 + level])
    half = LANES // 2
    shape = (LANES, LANES)
    shift = ((iota(shape, 0) + half == iota(shape, 1)) & (iota(shape, 0) < half)).astype(F32)
    shifted = dot(x, shift.astype(BF16)).astype(BF16)
    result = far_total[...]
    both = stack_two(x, shifted, down.shape[2])
    for pair in range(4):
        chain = dot(down[pair], both)
        upper = chain.astype(BF16)
        lower = (chain - upper.astype(F32)).astype(BF16)
        place = iota((2 * LANES, leaves), 0) % LANES
        goes = 8 * (place % half) + place // half + 2 * pair
        spot = (goes == iota((2 * LANES, leaves), 1)).astype(F32).astype(BF16)
        result = result + dot(jnp.concatenate([upper, lower], axis=1), spot)
    out_ref[...] = result[:coefs].astype(BF16)

    part = out_rows.at[pl.ds(0, (peers - 1) * slots)]
    pltpu.make_async_copy(part, part, a2a_send).wait()
    part = boxes.at[pl.ds(0, devices - 1)]
    pltpu.make_async_copy(part, part, box_send).wait()


def solution(mesh):
    sizes = (mesh.shape["gx"], mesh.shape["gy"], mesh.shape["gz"])
    peers = sizes[1] * sizes[2]
    devices = sizes[0] * peers

    def rows(table):
        return table.transpose(1, 0, 2).reshape(-1, table.shape[2])

    def on_device(mult, up, down, farw, send, src, kind, csrc, ckind):
        coefs, leaves = mult.shape
        kinds = farw.shape[0]
        slots = send.shape[3]
        sources = leaves + peers * slots
        tall = -(-coefs // 16) * 16
        wide = -(-coefs // LANES) * LANES
        vmem = pl.BlockSpec(memory_space=pltpu.VMEM)
        hbm = pl.BlockSpec(memory_space=pl.ANY)
        return pl.pallas_call(
            functools.partial(kernel, sizes),
            out_shape=jax.ShapeDtypeStruct((coefs, leaves), BF16),
            in_specs=[hbm] * 9,
            out_specs=vmem,
            scratch_shapes=[
                pltpu.VMEM((peers, slots), jnp.int32),
                pltpu.VMEM(src.shape, jnp.int32),
                pltpu.VMEM(kind.shape, jnp.int32),
                pltpu.SMEM(csrc.shape[::-1], jnp.int32),
                pltpu.SMEM(ckind.shape[::-1], jnp.int32),
                pltpu.VMEM(mult.shape, BF16),
                pltpu.VMEM((8 * coefs, coefs), BF16),
                pltpu.VMEM((8 * coefs, coefs), BF16),
                pltpu.VMEM((8 * coefs, coefs), BF16),
                pltpu.VMEM((4, tall, 2 * wide), BF16),
                pltpu.VMEM((4, tall, 2 * wide), BF16),
                pltpu.VMEM((4, tall, 2 * wide), BF16),
                pltpu.VMEM((leaves, 8 * LANES), BF16),
                pltpu.VMEM((LANES, 8 * LANES), BF16),
                pltpu.VMEM((peers * slots, wide), BF16),
                pltpu.VMEM((peers * slots, wide), BF16),
                pltpu.VMEM((kinds, sources, leaves), BF16),
                pltpu.VMEM((tall, sources), BF16),
                pltpu.VMEM((tall, leaves), F32),
                pltpu.VMEM((wide, LANES), F32),
                pltpu.VMEM((LANES, 8 * LANES), BF16),
                pltpu.VMEM((1, wide), F32),
                pltpu.VMEM((devices, 1, wide), F32),
                pltpu.SemaphoreType.DMA((9,)),
                pltpu.SemaphoreType.DMA,
                pltpu.SemaphoreType.DMA,
                pltpu.SemaphoreType.DMA,
                pltpu.SemaphoreType.DMA,
            ],
            compiler_params=pltpu.CompilerParams(
                collective_id=0, has_side_effects=True, vmem_limit_bytes=63 * 2**20
            ),
        )(
            mult,
            rows(up),
            rows(down),
            rows(farw),
            send.reshape(peers, slots),
            src,
            kind,
            csrc.T,
            ckind.T,
        )

    leaf = P(None, ("gx", "gy", "gz"))
    in_specs = (leaf, P(), P(), P(), P("gx", ("gy", "gz"), None, None), leaf, leaf, P(), P())
    return jax.shard_map(
        on_device, mesh=mesh, in_specs=in_specs, out_specs=leaf, check_vma=False
    )
```

```python
import functools

import jax
import jax.numpy as jnp
from jax import lax
from jax.experimental import pallas as pl
from jax.experimental.pallas import tpu as pltpu
from jax.sharding import PartitionSpec as P

MESH = pl.DeviceIdType.MESH
LOCAL_LEVELS = 3
LANES = 128
ROWS = 64
BLOCK = 32
FIELD = 15
LOW_NIBBLES = 0x0F0F0F0F
F32 = jnp.float32
BF16 = jnp.bfloat16


def iota(shape, dim):
    return lax.broadcasted_iota(jnp.int32, shape, dim)


def dot(a, b):
    return jnp.dot(a, b, preferred_element_type=F32)


def pick_children(rows):
    col = iota((1, 8 * LANES), 1)
    takes = 8 * (col % LANES) + col // LANES
    return (iota((rows, 8 * LANES), 0) == takes).astype(F32).astype(BF16)


def spread_children():
    col = iota((1, 8 * LANES), 1)
    place = col % LANES
    takes = jnp.where(place % 8 == col // LANES, place // 8, -1)
    return (iota((LANES, 8 * LANES), 0) == takes).astype(F32).astype(BF16)


def stack_two(first, second, depth):
    gap = jnp.zeros((depth // 2 - first.shape[0], first.shape[1]), BF16)
    return jnp.concatenate([first, gap, second, gap], axis=0)


def apply_eight(table, blocks):
    total = None
    for pair in range(4):
        first = blocks[:, 2 * pair * LANES : (2 * pair + 1) * LANES]
        second = blocks[:, (2 * pair + 1) * LANES : (2 * pair + 2) * LANES]
        term = dot(table[pair], stack_two(first, second, table.shape[2]))
        total = term if total is None else total + term
    return total


def octant_order():
    to = iota((8 * BLOCK, 1), 0)
    takes = 8 * (to % BLOCK) + to // BLOCK
    return (iota((8 * BLOCK, 8 * BLOCK), 1) == takes).astype(F32).astype(BF16)


def split_octants(raw, table, order, step):
    rows = raw[pl.ds(pl.multiple_of(step * 8 * BLOCK, 8 * BLOCK), 8 * BLOCK), :]
    out = dot(order[...], rows).astype(BF16)
    for c in range(8):
        spot = pl.ds(pl.multiple_of(step * BLOCK, BLOCK), BLOCK)
        at = c % 2 * (table.shape[2] // 2)
        table[c // 2, spot, at : at + out.shape[1]] = out[c * BLOCK : (c + 1) * BLOCK]


def split_tail(raw, table):
    coefs = raw.shape[0] // 8
    done = coefs // BLOCK * BLOCK
    left = coefs - done
    room = table.shape[1] - done
    shape = (8 * room, 8 * left)
    to, frm = iota(shape, 0), iota(shape, 1)
    hit = (frm == 8 * (to % room) + to // room) & (to % room < left)
    out = dot(hit.astype(F32).astype(BF16), raw[8 * done :, :]).astype(BF16)
    for c in range(8):
        at = c % 2 * (table.shape[2] // 2)
        table[c // 2, done:, at : at + out.shape[1]] = out[c * room : (c + 1) * room]


def kernel(
    sizes,
    mult_hbm,
    up_hbm,
    down_hbm,
    far_hbm,
    send_hbm,
    src_hbm,
    kind_hbm,
    csrc_hbm,
    ckind_hbm,
    out_ref,
    send_ref,
    src_ref,
    kind_ref,
    csrc_ref,
    ckind_ref,
    mult,
    up_raw,
    down_raw,
    far_raw,
    up,
    down,
    farw,
    sel,
    spread,
    out_rows,
    arrived,
    table,
    buf,
    far_total,
    turn,
    coarse_hot,
    order,
    message,
    boxes,
    load_sem,
    a2a_send,
    a2a_recv,
    box_send,
    box_recv,
):
    n_gx, n_gy, n_gz = sizes
    peers = n_gy * n_gz
    devices = n_gx * peers
    gx = lax.axis_index("gx")
    q = lax.axis_index("gy") * n_gz + lax.axis_index("gz")
    me = gx * peers + q
    coefs, leaves = mult.shape
    slots = send_ref.shape[1]
    kinds = table.shape[0]
    sources = table.shape[1]
    list_len = src_ref.shape[0]

    loads = [
        pltpu.make_async_copy(a, b, load_sem.at[i])
        for i, (a, b) in enumerate(
            (
                (up_hbm, up_raw),
                (mult_hbm, mult),
                (send_hbm, send_ref),
                (src_hbm, src_ref),
                (kind_hbm, kind_ref),
                (csrc_hbm, csrc_ref),
                (ckind_hbm, ckind_ref),
                (far_hbm, far_raw),
                (down_hbm, down_raw),
            )
        )
    ]
    for load in loads:
        load.start()

    def device_of(flat):
        return (flat // peers, (flat % peers) // n_gz, flat % n_gz)

    barrier = pltpu.get_barrier_semaphore()

    def greet(i, carry):
        pl.semaphore_signal(
            barrier, inc=1, device_id=device_of((me + i) % devices), device_id_type=MESH
        )
        return carry

    lax.fori_loop(1, devices, greet, 0)

    order[...] = octant_order()
    sel[...] = pick_children(leaves)
    spread[...] = spread_children()
    blocks = coefs // BLOCK
    half_depth = up.shape[2] // 2
    for one in (up, farw, down):
        for end in (half_depth, 2 * half_depth):
            one[:, :, end - LANES : end] = jnp.zeros(one.shape[:2] + (LANES,), BF16)
    buf[...] = jnp.zeros_like(buf)
    loads[0].wait()

    def split_up(i, carry):
        split_octants(up_raw, up, order, i)
        return carry

    lax.fori_loop(0, blocks, split_up, 0)
    split_tail(up_raw, up)
    loads[1].wait()
    turn[...] = jnp.zeros_like(turn)
    buf[:coefs, :leaves] = mult[...]
    x = buf[:, :leaves]
    for level in range(LOCAL_LEVELS):
        picked = dot(x, sel[: x.shape[1], :]).astype(BF16)
        total = apply_eight(up, picked)
        x = total.astype(BF16)
    turn[: x.shape[0], :] = x.astype(F32)
    row = turn[...].T[0:1, :]
    message[...] = row
    boxes[me] = row

    loads[2].wait()
    count = peers * slots
    row_of = (iota((count, peers), 0) // slots == iota((count, peers), 1)).astype(F32).astype(BF16)
    wanted = send_ref[...]
    upper = dot(row_of, (wanted // 32).astype(F32).astype(BF16))
    lower = dot(row_of, (wanted % 32).astype(F32).astype(BF16))
    mine = iota((count, slots), 0) % slots == iota((count, slots), 1)
    leaf = jnp.sum(jnp.where(mine, upper * 32.0 + lower, 0.0), axis=1, keepdims=True)
    hot = (leaf.astype(jnp.int32) == iota((count, leaves), 1)).astype(F32).astype(BF16)
    out_rows[...] = jnp.zeros_like(out_rows)
    out_rows[:, :coefs] = lax.dot_general(
        hot, mult[...], (((1,), (1,)), ((), ())), preferred_element_type=F32
    ).astype(BF16)
    own = pl.ds(pl.multiple_of(q * slots, slots), slots)
    arrived[own, :] = out_rows[own, :]

    pl.semaphore_wait(barrier, devices - 1)

    def send_box(i, carry):
        pltpu.make_async_remote_copy(
            src_ref=message,
            dst_ref=boxes.at[me],
            send_sem=box_send,
            recv_sem=box_recv,
            device_id=device_of((me + i) % devices),
            device_id_type=MESH,
        ).start()
        return carry

    lax.fori_loop(1, devices, send_box, 0)

    def send_rows(i, carry):
        other = (q + i) % peers
        pltpu.make_async_remote_copy(
            src_ref=out_rows.at[pl.ds(pl.multiple_of(other * slots, slots), slots)],
            dst_ref=arrived.at[own],
            send_sem=a2a_send,
            recv_sem=a2a_recv,
            device_id=(gx, other // n_gz, other % n_gz),
            device_id_type=MESH,
        ).start()
        return carry

    lax.fori_loop(1, peers, send_rows, 0)

    def count_rows(step, carry):
        s0 = pl.multiple_of(step * ROWS, ROWS)
        for lane in range(0, leaves, LANES):
            cols = slice(lane, lane + LANES)
            sid = iota((ROWS, LANES), 0) + s0
            parts = []
            for start in range(0, list_len, FIELD):
                acc = jnp.zeros((ROWS, LANES), jnp.int32)
                for j in range(start, min(start + FIELD, list_len)):
                    weight = kind_ref[j : j + 1, cols]
                    acc = acc + jnp.where(src_ref[j : j + 1, cols] == sid, weight, 0)
                parts.append(acc)
            even = sum(a & LOW_NIBBLES for a in parts)
            odd = sum(lax.shift_right_logical(a, 4) & LOW_NIBBLES for a in parts)
            for k in range(kinds):
                word = odd if k % 2 else even
                field = lax.shift_right_logical(word, 8 * (k // 2)) if k > 1 else word
                field = field & 255 if k < 6 else field
                table[k, pl.ds(s0, ROWS), cols] = field.astype(F32).astype(BF16)
        return carry

    def count_and_split(step, carry):
        split_octants(far_raw, farw, order, step)
        split_octants(down_raw, down, order, step)
        return count_rows(step, carry)

    for load in loads[3:]:
        load.wait()
    kind_ref[...] = lax.shift_left(jnp.int32(1), 4 * kind_ref[...])
    both = min(blocks, sources // ROWS)
    assert both == blocks
    lax.fori_loop(0, both, count_and_split, 0)
    lax.fori_loop(both, sources // ROWS, count_rows, 0)
    split_tail(far_raw, farw)
    split_tail(down_raw, down)

    box = me // 8
    total = jnp.zeros(coarse_hot.shape, jnp.int32)
    for j in range(csrc_ref.shape[1]):
        hit = (iota(total.shape, 0) == csrc_ref[box, j]) & (
            iota(total.shape, 1) == ckind_ref[box, j] * LANES
        )
        total = total + jnp.where(hit, 1, 0)
    coarse_hot[...] = total.astype(F32).astype(BF16)

    part = arrived.at[pl.ds(0, (peers - 1) * slots)]
    pltpu.make_async_copy(part, part, a2a_recv).wait()
    buf[:coefs, leaves:] = arrived[...].astype(F32).T[:coefs, :].astype(BF16)
    part = boxes.at[pl.ds(0, devices - 1)]
    pltpu.make_async_copy(part, part, box_recv).wait()
    far_total[...] = jnp.zeros_like(far_total)

    def add_kinds(which):
        for pair in which:
            first = dot(buf[...], table[2 * pair]).astype(BF16)
            second = dot(buf[...], table[2 * pair + 1]).astype(BF16)
            far_total[...] += dot(farw[pair], stack_two(first, second, farw.shape[2]))

    turns = [range(t * kinds // 8, (t + 1) * kinds // 8) for t in range(4)]

    x = boxes[...].reshape(devices, boxes.shape[2]).T[: buf.shape[0], :].astype(BF16)
    picked = dot(x, sel[:devices, :]).astype(BF16)
    coarse = apply_eight(up, picked).astype(BF16)
    add_kinds(turns[0])
    picked = dot(coarse, coarse_hot[...]).astype(BF16)
    x = apply_eight(farw, picked).astype(BF16)
    add_kinds(turns[1])

    octant = me % 8
    none = jnp.zeros_like(x)
    is_odd = octant % 2 == 1
    both = stack_two(jnp.where(is_odd, none, x), jnp.where(is_odd, x, none), down.shape[2])
    x = dot(down[octant // 2], both).astype(BF16)
    for level in range(LOCAL_LEVELS - 1):
        picked = dot(x, spread[...]).astype(BF16)
        x = apply_eight(down, picked).astype(BF16)
        add_kinds(turns[2 + level])
    half = LANES // 2
    shape = (LANES, LANES)
    shift = ((iota(shape, 0) + half == iota(shape, 1)) & (iota(shape, 0) < half)).astype(F32)
    shifted = dot(x, shift.astype(BF16)).astype(BF16)
    result = far_total[...]
    both = stack_two(x, shifted, down.shape[2])
    for pair in range(4):
        chain = dot(down[pair], both)
        upper = chain.astype(BF16)
        lower = (chain - upper.astype(F32)).astype(BF16)
        place = iota((2 * LANES, 1), 0) % LANES
        goes = 8 * (place % half) + place // half + 2 * pair
        spot = (goes == iota((2 * LANES, leaves), 1)).astype(F32).astype(BF16)
        result = result + dot(jnp.concatenate([upper, lower], axis=1), spot)
    out_ref[...] = result[:coefs].astype(BF16)

    part = out_rows.at[pl.ds(0, (peers - 1) * slots)]
    pltpu.make_async_copy(part, part, a2a_send).wait()
    part = boxes.at[pl.ds(0, devices - 1)]
    pltpu.make_async_copy(part, part, box_send).wait()


def solution(mesh):
    sizes = (mesh.shape["gx"], mesh.shape["gy"], mesh.shape["gz"])
    peers = sizes[1] * sizes[2]
    devices = sizes[0] * peers

    def rows(table):
        return table.transpose(1, 0, 2).reshape(-1, table.shape[2])

    def on_device(mult, up, down, farw, send, src, kind, csrc, ckind):
        coefs, leaves = mult.shape
        kinds = farw.shape[0]
        slots = send.shape[3]
        sources = leaves + peers * slots
        tall = -(-coefs // 16) * 16
        wide = -(-coefs // LANES) * LANES
        vmem = pl.BlockSpec(memory_space=pltpu.VMEM)
        hbm = pl.BlockSpec(memory_space=pl.ANY)
        return pl.pallas_call(
            functools.partial(kernel, sizes),
            out_shape=jax.ShapeDtypeStruct((coefs, leaves), BF16),
            in_specs=[hbm] * 9,
            out_specs=vmem,
            scratch_shapes=[
                pltpu.VMEM((peers, slots), jnp.int32),
                pltpu.VMEM(src.shape, jnp.int32),
                pltpu.VMEM(kind.shape, jnp.int32),
                pltpu.SMEM(csrc.shape[::-1], jnp.int32),
                pltpu.SMEM(ckind.shape[::-1], jnp.int32),
                pltpu.VMEM(mult.shape, BF16),
                pltpu.VMEM((8 * coefs, coefs), BF16),
                pltpu.VMEM((8 * coefs, coefs), BF16),
                pltpu.VMEM((8 * coefs, coefs), BF16),
                pltpu.VMEM((4, tall, 2 * wide), BF16),
                pltpu.VMEM((4, tall, 2 * wide), BF16),
                pltpu.VMEM((4, tall, 2 * wide), BF16),
                pltpu.VMEM((leaves, 8 * LANES), BF16),
                pltpu.VMEM((LANES, 8 * LANES), BF16),
                pltpu.VMEM((peers * slots, wide), BF16),
                pltpu.VMEM((peers * slots, wide), BF16),
                pltpu.VMEM((kinds, sources, leaves), BF16),
                pltpu.VMEM((tall, sources), BF16),
                pltpu.VMEM((tall, leaves), F32),
                pltpu.VMEM((wide, LANES), F32),
                pltpu.VMEM((LANES, 8 * LANES), BF16),
                pltpu.VMEM((8 * BLOCK, 8 * BLOCK), BF16),
                pltpu.VMEM((1, wide), F32),
                pltpu.VMEM((devices, 1, wide), F32),
                pltpu.SemaphoreType.DMA((9,)),
                pltpu.SemaphoreType.DMA,
                pltpu.SemaphoreType.DMA,
                pltpu.SemaphoreType.DMA,
                pltpu.SemaphoreType.DMA,
            ],
            compiler_params=pltpu.CompilerParams(
                collective_id=0, has_side_effects=True, vmem_limit_bytes=63 * 2**20
            ),
        )(
            mult,
            rows(up),
            rows(down),
            rows(farw),
            send.reshape(peers, slots),
            src,
            kind,
            csrc.T,
            ckind.T,
        )

    leaf = P(None, ("gx", "gy", "gz"))
    in_specs = (leaf, P(), P(), P(), P("gx", ("gy", "gz"), None, None), leaf, leaf, P(), P())
    return jax.shard_map(
        on_device, mesh=mesh, in_specs=in_specs, out_specs=leaf, check_vma=False
    )
```
